32 devices in a mesh: grp: 4 (over y, x), chan: 8 (over z, core).
Axes of the slice: x: 2, y: 2, z: 4, core: 2. Of those that a mesh axis runs over, the one named last changes fastest.
Arguments:
- voltages: bfloat16 [1024, 65536], P('grp', 'chan'), may hold values from -6 to 6
- prototype: float32 [8, 1024], replicated, may hold values from -2 to 2
Outputs:
- visibilities: bfloat16 [1024, 1024, 1024], P('chan', 'grp')
The draws below stay inside these ranges and needn't reach their ends.
All inputs are finite; a program needn't handle non-finite values.
Results may differ from the reference program's by a relative error of at most 0.0072.
Values may be sent and summed in bfloat16 or wider, within the bound.
No kernel may reach another device: no remote copies, remote signals or barrier semaphores. Data moves between devices by JAX's collectives and lax.ppermute only.
A program may use at most 128 MiB of HBM per device.

```python
import math
import jax
import jax.numpy as jnp
from jax import lax

INPUTS = 1024
K = 1024
TAPS = 8
FRAMES = 64
SAMPLES = 65536


def levels(stream_key, dims, cuts, low, top_value):
    loudness, own = 1.0, jax.random.fold_in(stream_key, 6)
    for position, blocks in cuts:
        steps = jnp.exp(jax.random.uniform(jax.random.fold_in(own, position), (blocks,), jnp.float32, low / len(cuts), top_value / len(cuts)))
        loudness = loudness * jnp.repeat(steps, dims[position] // blocks).reshape([-1 if axis == position else 1 for axis in range(len(dims))])
    return loudness


def bell_draw(own_key, shape, scale, reach, cuts=(), kind=jnp.bfloat16):
    result = jax.random.normal(own_key, shape, jnp.float32) * scale
    if len(cuts) > 0:
        result = levels(own_key, shape, cuts, -0.22, 0.18) * result
    return jnp.clip(result, min=-reach, max=reach).astype(kind)


def setup_inputs(seed: int = 0) -> dict:
    splits = jax.random.split(jax.random.key(seed), 3)
    return {
        "voltages": bell_draw(splits[0], (INPUTS, SAMPLES), 1.0, 6.0, ((0, 4), (1, 8))),
        "prototype": bell_draw(splits[1], (TAPS, K), 0.35, 2.0, (), jnp.float32),
    }


def cosine_table(width):
    places = jnp.arange(width, dtype=jnp.int32)
    phase = (2 * places[:, None] + 1) * (2 * places[None, :] + 1) % (8 * width)
    return jnp.cos(phase.astype(jnp.float32) * (math.pi / (4 * width))).astype(jnp.bfloat16)

def fold_frames(extended, prototype, count):
    total = jnp.zeros((extended.shape[0], count, extended.shape[2]), jnp.float32)
    for tap_index in range(prototype.shape[0]):
        parity = 1.0 if tap_index % 2 == 0 else -1.0
        weights = parity * prototype[tap_index]
        total = total + weights[None, None, :] * extended[:, tap_index:tap_index + count].astype(jnp.float32)
    return total.astype(jnp.bfloat16)

def reference(voltages, prototype):
    framed = voltages.reshape(INPUTS, FRAMES, K)
    padded = jnp.concatenate([framed, jnp.zeros((INPUTS, TAPS - 1, K), jnp.bfloat16)], axis=1)
    table = cosine_table(K)
    blocked = padded.reshape(INPUTS // 64, 64, FRAMES + TAPS - 1, K)

    def spectra_block(extended):
        folded = fold_frames(extended, prototype, FRAMES)
        product = jnp.einsum('itm,mk->kti', folded.astype(jnp.float32), table.astype(jnp.float32))
        return (product * math.sqrt(2.0 / K)).astype(jnp.bfloat16)
    pieces = lax.map(spectra_block, blocked)
    spectra = jnp.transpose(pieces, (1, 2, 0, 3)).reshape(K, FRAMES, INPUTS)
    grouped = spectra.reshape(K // 16, 16, FRAMES, INPUTS)

    def correlate(block):
        wide = block.astype(jnp.float32)
        return (jnp.einsum('cti,ctj->cij', wide, wide) / FRAMES).astype(jnp.bfloat16)
    return lax.map(correlate, grouped).reshape(K, INPUTS, INPUTS)
```

```python
import functools
import math

import jax
import jax.numpy as jnp
from jax import lax
from jax.experimental import pallas as pl
from jax.experimental.pallas import tpu as pltpu
from jax.sharding import PartitionSpec as P

BOUNDS = (0, 11, 16)
CALLS = ((0, 6, 11), (11, 16))
ROW_STEPS = 4
PAIRS = 2
FOLD_VMEM = 28 * 1024 * 1024
CORRELATE_VMEM = 60 * 1024 * 1024


def swap(block, axis, bit):
    return lax.ppermute(block, axis, [(i, i ^ bit) for i in range(lax.axis_size(axis))])


def after(value, *events):
    return lax.optimization_barrier((value,) + events)[0]


def cosine_rows(starts, count, width):
    fine = math.gcd(count, 32)
    places = 2 * jnp.arange(width, dtype=jnp.int32)[None, :] + 1
    turns = lambda steps: (steps[:, None] * places % (8 * width)).astype(jnp.float32) * (
        math.pi / (4 * width)
    )
    blocks = starts[:, None] + fine * jnp.arange(count // fine, dtype=jnp.int32)[None, :]
    coarse_turn = turns(2 * blocks.reshape(-1))
    fine_turn = turns(2 * jnp.arange(fine, dtype=jnp.int32) + 1)
    trig = [jnp.cos(coarse_turn), jnp.sin(coarse_turn), jnp.cos(fine_turn), jnp.sin(fine_turn)]
    cos_a, sin_a, cos_b, sin_b = lax.optimization_barrier(trig)
    table = cos_a[:, None] * cos_b[None] - sin_a[:, None] * sin_b[None]
    return table.reshape(-1, width).astype(jnp.bfloat16)


def spectra_kernel(late, cuts, scale, core_ref, weights_ref, table_ref, *refs):
    sources = 4 if late else 2
    inputs, outs = refs[:sources], refs[sources:-4]
    samples, folded, spread, sems = refs[-4:]
    core = core_ref[0]
    own, other = inputs[0], inputs[1]
    count, width = folded.shape[1], folded.shape[2]
    depth, frames = weights_ref.shape[0], folded.shape[0]
    slab, tail = frames * width, (depth - 1) * width
    step_rows = count // ROW_STEPS
    half_rows = count // 2

    def slab_copy(ref, step, columns, start, which):
        rows = pl.ds(step * step_rows, step_rows)
        return pltpu.make_async_copy(
            ref.at[rows, pl.ds(0, columns)],
            samples.at[rows, pl.ds(start, columns)],
            sems.at[which, step],
        )

    def halo_copy(ref, step):
        rows = pl.ds(step * step_rows, step_rows)
        return pltpu.make_async_copy(
            ref.at[pl.ds(step * step_rows % half_rows, step_rows), :],
            samples.at[rows, pl.ds(slab, tail)],
            sems.at[1, step],
        )

    def start_all(first, second):
        for step in range(ROW_STEPS):
            slab_copy(first, step, slab, 0, 0).start()
            if not late:
                slab_copy(second, step, tail, slab, 1).start()

    head_core = 1 if late else 0

    @pl.when(core == head_core)
    def _():
        start_all(own, other)

    @pl.when(core != head_core)
    def _():
        start_all(other, own)

    if late:
        for step in range(ROW_STEPS):
            half = step * step_rows // half_rows

            @pl.when(core == half)
            def _():
                halo_copy(inputs[2], step).start()

            @pl.when(core != half)
            def _():
                halo_copy(inputs[3], step).start()

    for step in range(ROW_STEPS):
        slab_copy(own, step, slab, 0, 0).wait()
        if late:
            halo_copy(inputs[2], step).wait()
        else:
            slab_copy(own, step, tail, slab, 1).wait()

        def fold(tile, carry):
            lanes = pl.multiple_of(tile * 128, 128)
            taps = [
                jnp.broadcast_to(weights_ref[pl.ds(tap, 1), pl.ds(lanes, 128)], (16, 128))
                for tap in range(depth)
            ]
            for block in range(step_rows // 16):
                rows = pl.ds(step * step_rows + block * 16, 16)
                window = [
                    samples[rows, pl.ds(pl.multiple_of(lanes + place * width, 128), 128)].astype(
                        jnp.float32
                    )
                    for place in range(frames + depth - 1)
                ]
                for frame in range(frames):
                    total = taps[0] * window[frame]
                    for tap in range(1, depth):
                        total = total + taps[tap] * window[frame + tap]
                    folded[frame, rows, pl.ds(lanes, 128)] = total.astype(jnp.bfloat16)
            return carry

        lax.fori_loop(0, width // 128, fold, 0)

    channels = table_ref.shape[0]
    for frame in range(frames):
        product = scale * lax.dot_general(
            table_ref[...],
            folded[frame],
            (((1,), (1,)), ((), ())),
            preferred_element_type=jnp.float32,
        )
        for half in range(count // 128):
            spread[half, pl.ds(frame, channels, stride=frames), :] = product[
                :, half * 128 : half * 128 + 128
            ]
    for (first, rows), out in zip(cuts, outs):
        for half in range(count // 128):
            out[:, half * 128 : half * 128 + 128] = spread[half, first : first + rows, :].astype(
                jnp.bfloat16
            )


def spectra_blocks(late, cuts, core, weights, table, sources):
    count = sources[0].shape[0]
    depth, width = weights.shape
    frames = sources[0].shape[1] // width
    channels = table.shape[0]
    cuts = [(first * frames, rows * frames) for first, rows in cuts]
    whole = pl.BlockSpec(memory_space=pltpu.VMEM)
    return pl.pallas_call(
        functools.partial(spectra_kernel, late, cuts, math.sqrt(2.0 / width)),
        out_shape=[jax.ShapeDtypeStruct((rows, count), jnp.bfloat16) for _, rows in cuts],
        in_specs=[pl.BlockSpec(memory_space=pltpu.SMEM), whole, whole]
        + [pl.BlockSpec(memory_space=pl.ANY)] * len(sources),
        out_specs=[whole] * len(cuts),
        scratch_shapes=[
            pltpu.VMEM((count, (frames + depth - 1) * width), jnp.bfloat16),
            pltpu.VMEM((frames, count, width), jnp.bfloat16),
            pltpu.VMEM((count // 128, channels * frames, 128), jnp.float32),
            pltpu.SemaphoreType.DMA((2, ROW_STEPS)),
        ],
        compiler_params=pltpu.CompilerParams(vmem_limit_bytes=FOLD_VMEM),
        cost_estimate=pl.CostEstimate(flops=1, bytes_accessed=1, transcendentals=0),
        name="fold_transform",
    )(core, weights, table, *sources)


def correlate_kernel(scale, groups, ordered, first, group_ref, *refs):
    out, held, sems = refs[-3:]
    count = out.shape[1]
    group = group_ref[0]
    step, steps = pl.program_id(0), pl.num_programs(0)
    slot = step % 2
    pieces, used = [], 0
    for is_ordered in ordered:
        members = refs[used : used + (1 if is_ordered else groups)]
        used += len(members)
        pieces += [(is_ordered, members, part) for part in range(members[0].shape[-3])]

    def copy(where, channel):
        target = first + step * 2 * PAIRS + channel
        return pltpu.make_async_copy(held.at[where, channel], out.at[target], sems.at[where, channel])

    def wait_all(where):
        for channel in range(2 * PAIRS):
            copy(where, channel).wait()

    @pl.when(step >= 2)
    def _():
        wait_all(slot)

    depth = len(pieces) * 16
    places = lax.broadcasted_iota(jnp.int32, (count, depth), 1)
    even = jnp.where(places % 16 < 8, scale, 0.0).astype(jnp.bfloat16)
    odd = jnp.where(places % 16 < 8, 0.0, scale).astype(jnp.bfloat16)
    for pair in range(PAIRS):
        rows = slice(pair * 16, pair * 16 + 16)

        def stack(member):
            return jnp.concatenate(
                [
                    members[0][group ^ member, part, rows, :]
                    if is_ordered
                    else members[member][part, rows, :]
                    for is_ordered, members, part in pieces
                ],
                axis=0,
            )

        turned = stack(0).T
        left = jnp.concatenate([turned * even, turned * odd], axis=0)
        for member in range(groups):
            summed = lax.dot_general(
                left, stack(member), (((1,), (0,)), ((), ())), preferred_element_type=jnp.float32
            )
            columns = pl.ds(pl.multiple_of((group ^ member) * count, 128), count)
            result = summed.astype(jnp.bfloat16)
            held[slot, 2 * pair, :, columns] = result[:count]
            held[slot, 2 * pair + 1, :, columns] = result[count:]
        copy(slot, 2 * pair).start()
        copy(slot, 2 * pair + 1).start()

    @pl.when(step == steps - 1)
    def _():
        wait_all(slot)

    @pl.when((step == steps - 1) & (steps > 1))
    def _():
        wait_all(1 - slot)


def correlate(frames, first, stop, start, channels, group, wide, narrow, earlier):
    groups, count = lax.axis_size("grp"), (wide + narrow)[0][-1].shape[-1]
    block = 2 * PAIRS
    base, steps = first // block, (stop - first) // block
    pieces = [(piece, base) for piece in wide] + [
        (piece, (first - start) // block) for piece in narrow
    ]
    ordered = [len(piece) == 1 for piece, _ in pieces]
    operands = [array for piece, _ in pieces for array in piece]
    aliases = {} if earlier is None else {1 + len(operands): 0}
    carried = [] if earlier is None else [earlier]

    def spec(array, start):
        if len(array.shape) == 4:
            return pl.BlockSpec(
                (groups, array.shape[1], 16 * PAIRS, count), lambda i, ref: (0, 0, start + i, 0)
            )
        return pl.BlockSpec((array.shape[0], 16 * PAIRS, count), lambda i, ref: (0, start + i, 0))

    return pl.pallas_call(
        functools.partial(correlate_kernel, 1.0 / frames, groups, ordered, first),
        out_shape=jax.ShapeDtypeStruct((channels, count, groups * count), jnp.bfloat16),
        grid_spec=pltpu.PrefetchScalarGridSpec(
            num_scalar_prefetch=1,
            grid=(steps,),
            in_specs=[spec(array, start) for piece, start in pieces for array in piece]
            + [pl.BlockSpec(memory_space=pl.ANY)] * len(carried),
            out_specs=pl.BlockSpec(memory_space=pl.ANY),
            scratch_shapes=[
                pltpu.VMEM((2, block, count, groups * count), jnp.bfloat16),
                pltpu.SemaphoreType.DMA((2, block)),
            ],
        ),
        input_output_aliases=aliases,
        compiler_params=pltpu.CompilerParams(vmem_limit_bytes=CORRELATE_VMEM),
        cost_estimate=pl.CostEstimate(flops=1, bytes_accessed=1, transcendentals=0),
        name="correlate",
    )(group, *operands, *carried)


def joined(block, turn, earlier=(), events=()):
    groups = lax.axis_size("grp")
    bits = [1 << b for b in range(groups.bit_length() - 1)]
    bits = bits[turn % len(bits) :] + bits[: turn % len(bits)]
    held = {bit: swap(after(block, *earlier), "grp", bit) for bit in bits}
    direct = tuple(held[bit] for bit in bits)
    reached = bits[:1]
    for bit in bits[1:]:
        for member in list(reached):
            held[member | bit] = swap(after(held[member], *direct, *events), "grp", bit)
        reached += [bit] + [member | bit for member in reached]
    held[0] = block
    return [held[member] for member in range(groups)], direct


def on_device(voltages, prototype):
    depth, width = prototype.shape
    owners = lax.axis_size("chan")
    parts = owners // 2
    channels = width // owners
    frames_here = voltages.shape[1] // width
    frames = frames_here * owners
    place = lax.axis_index("chan")
    core = place % 2
    group = lax.axis_index("grp")
    half = voltages.shape[0] // 2

    other = swap(voltages, "chan", 1)
    route = [[(2 * p + 2, 2 * p + k) for p in range(parts - 1)] for k in (0, 1)]
    tail = (depth - 1) * width
    sliced = [voltages[k * half : k * half + half, :tail] for k in (0, 1)]
    ahead = [lax.ppermute(sliced[k], "chan", route[k]) for k in (0, 1)]
    other = after(other, *sliced)

    owned = (place // 2) ^ jnp.arange(parts, dtype=jnp.int32)
    table = cosine_rows((owned * 2 + core) * channels, channels, width)
    signs = jnp.where(jnp.arange(depth) % 2 == 0, 1.0, -1.0).astype(jnp.float32)
    weights = signs[:, None] * prototype
    at_core = core.reshape(1)

    bounds = [round(channels * bound / 64) * 4 for bound in BOUNDS]
    blocks = list(zip(bounds[:-1], bounds[1:]))
    cuts = [(0, channels), (channels, channels)] + [
        (part * channels + first, stop - first) for first, stop in blocks for part in range(2, parts)
    ]
    early = spectra_blocks(False, cuts, at_core, weights, table, [voltages, other])
    own_early, sent = joined(early[0][None], 0)
    ahead = lax.optimization_barrier((ahead[0], ahead[1], *own_early[1:]))
    halo = jnp.where(core == 0, ahead[0], ahead[1])
    other_halo = swap(halo, "chan", 1)

    near = swap(after(early[1], ahead[0], ahead[1]), "chan", 2)
    early_parts = [early[2 + i * (parts - 2) :][: parts - 2] for i in range(len(blocks))]
    middle = swap(after(early_parts[0][0], ahead[0], ahead[1]), "chan", 4)
    near, middle = lax.optimization_barrier((near, middle))
    near_joined, sent = joined(near[None], 1, sent)

    cuts = [(first, stop - first) for first, stop in blocks] + [
        (part * channels + first, stop - first) for first, stop in blocks for part in range(1, parts)
    ]
    late = spectra_blocks(
        True, cuts, at_core, weights, table, [voltages, other, halo, after(other_halo, near)]
    )
    moved, landed = [], ()
    for index in range(len(blocks)):
        if index > 0:
            middle = swap(after(early_parts[index][0], *landed), "chan", 4)
        waits = (middle,) if index == 0 else landed
        far = [
            swap(after(early_parts[index][part - 2], *waits), "chan", 2 * part)
            for part in range(3, parts)
        ]
        late_parts = late[len(blocks) + index * (parts - 1) :][: parts - 1]
        hops = [
            swap(after(late_parts[part - 1], middle, *far), "chan", 2 * part)
            for part in range(1, parts)
        ]
        landed = tuple(hops)
        moved.append((jnp.stack([late[index], middle] + far), jnp.stack(hops)))

    wide, results = [own_early, near_joined], [None]
    for index, (first, stop) in enumerate(blocks):
        ready, own_sent = joined(moved[index][0], 0, sent, results[1:2])
        if index == 0:
            sent = own_sent + tuple(near_joined[1:])
        rest, own_sent = joined(
            moved[index][1], 1, sent, results[1:2] if index > 0 else landed
        )
        sent = own_sent
        calls = [round(channels * bound / 64) * 4 for bound in CALLS[index]]
        for call_first, call_stop in zip(calls[:-1], calls[1:]):
            results.append(
                correlate(
                    frames,
                    call_first,
                    call_stop,
                    first,
                    channels,
                    group.reshape(1),
                    wide,
                    [ready, rest],
                    results[-1],
                )
            )
    return results[-1]


def solution(mesh):
    placed = (P("grp", "chan"), P())
    return jax.shard_map(
        on_device, mesh=mesh, in_specs=placed, out_specs=P("chan", "grp", None), check_vma=False
    )
```

```python
import functools
import math

import jax
import jax.numpy as jnp
from jax import lax
from jax.experimental import pallas as pl
from jax.experimental.pallas import tpu as pltpu
from jax.sharding import PartitionSpec as P

BOUNDS = (0, 6, 11, 16)
ROW_STEPS = 4
PAIRS = 2
FOLD_VMEM = 28 * 1024 * 1024
CORRELATE_VMEM = 60 * 1024 * 1024


def swap(block, axis, bit):
    return lax.ppermute(block, axis, [(i, i ^ bit) for i in range(lax.axis_size(axis))])


def after(value, *events):
    return lax.optimization_barrier((value,) + events)[0]


def cosine_rows(starts, count, width):
    fine = math.gcd(count, 32)
    places = 2 * jnp.arange(width, dtype=jnp.int32)[None, :] + 1
    turns = lambda steps: (steps[:, None] * places % (8 * width)).astype(jnp.float32) * (
        math.pi / (4 * width)
    )
    blocks = starts[:, None] + fine * jnp.arange(count // fine, dtype=jnp.int32)[None, :]
    coarse_turn = turns(2 * blocks.reshape(-1))
    fine_turn = turns(2 * jnp.arange(fine, dtype=jnp.int32) + 1)
    trig = [jnp.cos(coarse_turn), jnp.sin(coarse_turn), jnp.cos(fine_turn), jnp.sin(fine_turn)]
    cos_a, sin_a, cos_b, sin_b = lax.optimization_barrier(trig)
    table = cos_a[:, None] * cos_b[None] - sin_a[:, None] * sin_b[None]
    return table.reshape(-1, width).astype(jnp.bfloat16)


def spectra_kernel(late, cuts, scale, core_ref, weights_ref, table_ref, *refs):
    sources = 6 if late else 2
    inputs, outs = refs[:sources], refs[sources:-4]
    samples, folded, spread, sems = refs[-4:]
    core = core_ref[0]
    own, other = inputs[0], inputs[1]
    count, width = folded.shape[1], folded.shape[2]
    depth, frames = weights_ref.shape[0], folded.shape[0]
    slab, tail = frames * width, (depth - 1) * width
    step_rows = count // ROW_STEPS
    half_rows = count // 2

    def slab_copy(ref, step, columns, start, which):
        rows = pl.ds(step * step_rows, step_rows)
        return pltpu.make_async_copy(
            ref.at[rows, pl.ds(0, columns)],
            samples.at[rows, pl.ds(start, columns)],
            sems.at[which, step],
        )

    def halo_copy(refs, step, which):
        rows = pl.ds(step * step_rows, step_rows)
        start = slab + which * refs[0].shape[1]
        return pltpu.make_async_copy(
            refs[which].at[pl.ds(step * step_rows % half_rows, step_rows), :],
            samples.at[rows, pl.ds(start, refs[which].shape[1])],
            sems.at[1 + which, step],
        )

    def start_all(first, second):
        for step in range(ROW_STEPS):
            slab_copy(first, step, slab, 0, 0).start()
            if not late:
                slab_copy(second, step, tail, slab, 1).start()

    head_core = 1 if late else 0

    @pl.when(core == head_core)
    def _():
        start_all(own, other)

    @pl.when(core != head_core)
    def _():
        start_all(other, own)

    if late:
        for step in range(ROW_STEPS):
            half = step * step_rows // half_rows

            @pl.when(core == half)
            def _():
                halo_copy(inputs[2:4], step, 0).start()
                halo_copy(inputs[2:4], step, 1).start()

            @pl.when(core != half)
            def _():
                halo_copy(inputs[4:6], step, 0).start()
                halo_copy(inputs[4:6], step, 1).start()

    for step in range(ROW_STEPS):
        slab_copy(own, step, slab, 0, 0).wait()
        if late:
            halo_copy(inputs[2:4], step, 0).wait()
            halo_copy(inputs[2:4], step, 1).wait()
        else:
            slab_copy(own, step, tail, slab, 1).wait()

        def fold(tile, carry):
            lanes = pl.multiple_of(tile * 128, 128)
            taps = [
                jnp.broadcast_to(weights_ref[pl.ds(tap, 1), pl.ds(lanes, 128)], (16, 128))
                for tap in range(depth)
            ]
            for block in range(step_rows // 16):
                rows = pl.ds(step * step_rows + block * 16, 16)
                window = [
                    samples[rows, pl.ds(pl.multiple_of(lanes + place * width, 128), 128)].astype(
                        jnp.float32
                    )
                    for place in range(frames + depth - 1)
                ]
                for frame in range(frames):
                    total = taps[0] * window[frame]
                    for tap in range(1, depth):
                        total = total + taps[tap] * window[frame + tap]
                    folded[frame, rows, pl.ds(lanes, 128)] = total.astype(jnp.bfloat16)
            return carry

        lax.fori_loop(0, width // 128, fold, 0)

    channels = table_ref.shape[0]
    for frame in range(frames):
        product = scale * lax.dot_general(
            table_ref[...],
            folded[frame],
            (((1,), (1,)), ((), ())),
            preferred_element_type=jnp.float32,
        )
        for half in range(count // 128):
            spread[half, pl.ds(frame, channels, stride=frames), :] = product[
                :, half * 128 : half * 128 + 128
            ]
    for (first, rows), out in zip(cuts, outs):
        for half in range(count // 128):
            out[:, half * 128 : half * 128 + 128] = spread[half, first : first + rows, :].astype(
                jnp.bfloat16
            )


def spectra_blocks(late, cuts, core, weights, table, sources):
    count = sources[0].shape[0]
    depth, width = weights.shape
    frames = sources[0].shape[1] // width
    channels = table.shape[0]
    cuts = [(first * frames, rows * frames) for first, rows in cuts]
    whole = pl.BlockSpec(memory_space=pltpu.VMEM)
    return pl.pallas_call(
        functools.partial(spectra_kernel, late, cuts, math.sqrt(2.0 / width)),
        out_shape=[jax.ShapeDtypeStruct((rows, count), jnp.bfloat16) for _, rows in cuts],
        in_specs=[pl.BlockSpec(memory_space=pltpu.SMEM), whole, whole]
        + [pl.BlockSpec(memory_space=pl.ANY)] * len(sources),
        out_specs=[whole] * len(cuts),
        scratch_shapes=[
            pltpu.VMEM((count, (frames + depth - 1) * width), jnp.bfloat16),
            pltpu.VMEM((frames, count, width), jnp.bfloat16),
            pltpu.VMEM((count // 128, channels * frames, 128), jnp.float32),
            pltpu.SemaphoreType.DMA((3, ROW_STEPS)),
        ],
        compiler_params=pltpu.CompilerParams(vmem_limit_bytes=FOLD_VMEM),
        cost_estimate=pl.CostEstimate(flops=1, bytes_accessed=1, transcendentals=0),
        name="fold_transform",
    )(core, weights, table, *sources)


def correlate_kernel(scale, groups, ordered, first, group_ref, *refs):
    out, held, sems = refs[-3:]
    count = out.shape[1]
    group = group_ref[0]
    step, steps = pl.program_id(0), pl.num_programs(0)
    slot = step % 2
    pieces, used = [], 0
    for is_ordered in ordered:
        members = refs[used : used + (1 if is_ordered else groups)]
        used += len(members)
        pieces += [(is_ordered, members, part) for part in range(members[0].shape[-3])]

    def copy(where, channel):
        target = first + step * 2 * PAIRS + channel
        return pltpu.make_async_copy(held.at[where, channel], out.at[target], sems.at[where, channel])

    def wait_all(where):
        for channel in range(2 * PAIRS):
            copy(where, channel).wait()

    @pl.when(step >= 2)
    def _():
        wait_all(slot)

    depth = len(pieces) * 16
    places = lax.broadcasted_iota(jnp.int32, (count, depth), 1)
    even = jnp.where(places % 16 < 8, 1.0, 0.0).astype(jnp.bfloat16)
    odd = jnp.where(places % 16 < 8, 0.0, 1.0).astype(jnp.bfloat16)
    for pair in range(PAIRS):
        rows = slice(pair * 16, pair * 16 + 16)

        def stack(member):
            return jnp.concatenate(
                [
                    members[0][group ^ member, part, rows, :]
                    if is_ordered
                    else members[member][part, rows, :]
                    for is_ordered, members, part in pieces
                ],
                axis=0,
            )

        turned = stack(0).T
        left = jnp.concatenate([turned * even, turned * odd], axis=0)
        for member in range(groups):
            summed = scale * lax.dot_general(
                left, stack(member), (((1,), (0,)), ((), ())), preferred_element_type=jnp.float32
            )
            columns = pl.ds(pl.multiple_of((group ^ member) * count, 128), count)
            result = summed.astype(jnp.bfloat16)
            held[slot, 2 * pair, :, columns] = result[:count]
            held[slot, 2 * pair + 1, :, columns] = result[count:]
        copy(slot, 2 * pair).start()
        copy(slot, 2 * pair + 1).start()

    @pl.when(step == steps - 1)
    def _():
        wait_all(slot)

    @pl.when((step == steps - 1) & (steps > 1))
    def _():
        wait_all(1 - slot)


def correlate(frames, first, stop, channels, group, wide, narrow, earlier):
    groups, count = lax.axis_size("grp"), (wide + narrow)[0][-1].shape[-1]
    block = 2 * PAIRS
    base, steps = first // block, (stop - first) // block
    pieces = [(piece, base) for piece in wide] + [(piece, 0) for piece in narrow]
    ordered = [len(piece) == 1 for piece, _ in pieces]
    operands = [array for piece, _ in pieces for array in piece]
    aliases = {} if earlier is None else {1 + len(operands): 0}
    carried = [] if earlier is None else [earlier]

    def spec(array, start):
        if len(array.shape) == 4:
            return pl.BlockSpec(
                (groups, array.shape[1], 16 * PAIRS, count), lambda i, ref: (0, 0, start + i, 0)
            )
        return pl.BlockSpec((array.shape[0], 16 * PAIRS, count), lambda i, ref: (0, start + i, 0))

    return pl.pallas_call(
        functools.partial(correlate_kernel, 1.0 / frames, groups, ordered, first),
        out_shape=jax.ShapeDtypeStruct((channels, count, groups * count), jnp.bfloat16),
        grid_spec=pltpu.PrefetchScalarGridSpec(
            num_scalar_prefetch=1,
            grid=(steps,),
            in_specs=[spec(array, start) for piece, start in pieces for array in piece]
            + [pl.BlockSpec(memory_space=pl.ANY)] * len(carried),
            out_specs=pl.BlockSpec(memory_space=pl.ANY),
            scratch_shapes=[
                pltpu.VMEM((2, block, count, groups * count), jnp.bfloat16),
                pltpu.SemaphoreType.DMA((2, block)),
            ],
        ),
        input_output_aliases=aliases,
        compiler_params=pltpu.CompilerParams(vmem_limit_bytes=CORRELATE_VMEM),
        cost_estimate=pl.CostEstimate(flops=1, bytes_accessed=1, transcendentals=0),
        name="correlate",
    )(group, *operands, *carried)


def joined(block, turn, earlier=None, events=()):
    groups = lax.axis_size("grp")
    bits = [1 << b for b in range(groups.bit_length() - 1)]
    bits = bits[turn % len(bits) :] + bits[: turn % len(bits)]
    held = {0: block}
    for bit in bits:
        for member in list(held):
            waits = () if earlier is None else (earlier[member | bit],)
            sent = after(held[member], *waits, *(events if member else ()))
            held[member | bit] = swap(sent, "grp", bit)
    return [held[member] for member in range(groups)]


def on_device(voltages, prototype):
    depth, width = prototype.shape
    owners = lax.axis_size("chan")
    parts = owners // 2
    channels = width // owners
    frames_here = voltages.shape[1] // width
    frames = frames_here * owners
    place = lax.axis_index("chan")
    core = place % 2
    group = lax.axis_index("grp")
    half = voltages.shape[0] // 2

    other = swap(voltages, "chan", 1)
    route = [[(2 * p + 2, 2 * p + k) for p in range(parts - 1)] for k in (0, 1)]
    tail = (depth - 1) * width
    split = width * ((depth - 1) // 2)

    def ahead_of(first, stop, *events):
        return [
            lax.ppermute(
                after(voltages[k * half : k * half + half, first:stop], *events), "chan", route[k]
            )
            for k in (0, 1)
        ]

    def swapped(pair):
        mine = jnp.where(core == 0, pair[0], pair[1])
        return mine, swap(mine, "chan", 1)

    ahead = ahead_of(0, split)

    owned = (place // 2) ^ jnp.arange(parts, dtype=jnp.int32)
    table = cosine_rows((owned * 2 + core) * channels, channels, width)
    signs = jnp.where(jnp.arange(depth) % 2 == 0, 1.0, -1.0).astype(jnp.float32)
    weights = signs[:, None] * prototype
    at_core = core.reshape(1)

    cuts = [(part * channels, channels) for part in range(parts)]
    early = spectra_blocks(False, cuts, at_core, weights, table, [voltages, other])
    own_early = joined(early[0][None], 0)
    near = swap(after(early[1], *ahead), "chan", 2)
    middle = swap(after(early[2], *ahead), "chan", 4)
    near_joined = joined(near[None], 1, own_early)
    middle_joined = joined(middle[None], 0, near_joined)
    rest = ahead_of(split, tail, near, middle, *own_early[1:3])
    far = [swap(after(early[part], *rest), "chan", 2 * part) for part in range(3, parts)]
    halo, other_halo = swapped(ahead)
    rest = lax.optimization_barrier((*rest, *middle_joined[1:3]))[:2]
    halo_rest, other_rest = swapped(rest)
    sources = [voltages, other, halo, halo_rest, other_halo, other_rest]
    bounds = [round(channels * bound / 64) * 4 for bound in BOUNDS]
    blocks = list(zip(bounds[:-1], bounds[1:]))
    cuts = [(0, channels)] + [
        (part * channels + first, stop - first)
        for first, stop in blocks
        for part in range(1, parts)
    ]
    late = spectra_blocks(True, cuts, at_core, weights, table, sources)
    own_late = joined(late[0][None], 1, middle_joined)
    far_joined = joined(jnp.stack(far), 0, own_late)
    wide = [own_early, near_joined, middle_joined, own_late, far_joined]
    landed, narrow, results = [near, middle] + far, [far_joined], [None]
    for chunk, (first, stop) in enumerate(blocks):
        skipped = chunk * (parts - 1)
        landed = [
            swap(after(late[skipped + part], landed[part - 1]), "chan", 2 * part)
            for part in range(1, parts)
        ]
        events = results[chunk - 1 : chunk] if chunk >= 2 else ()
        narrow.append(joined(jnp.stack(landed), chunk + 1, narrow[-1], events))
        results.append(
            correlate(
                frames, first, stop, channels, group.reshape(1), wide, [narrow[-1]], results[-1]
            )
        )
    return results[-1]


def solution(mesh):
    placed = (P("grp", "chan"), P())
    return jax.shard_map(
        on_device, mesh=mesh, in_specs=placed, out_specs=P("chan", "grp", None), check_vma=False
    )
```

```python
import functools
import math

import jax
import jax.numpy as jnp
from jax import lax
from jax.experimental import pallas as pl
from jax.experimental.pallas import tpu as pltpu
from jax.sharding import PartitionSpec as P

BOUNDS = (0, 6, 11, 16)
ROW_STEPS = 4
PAIRS = 4
FOLD_VMEM = 28 * 1024 * 1024
CORRELATE_VMEM = 60 * 1024 * 1024


def swap(block, axis, bit):
    return lax.ppermute(block, axis, [(i, i ^ bit) for i in range(lax.axis_size(axis))])


def after(value, *events):
    return lax.optimization_barrier((value,) + events)[0]


def cosine_rows(starts, count, width):
    fine = math.gcd(count, 32)
    places = 2 * jnp.arange(width, dtype=jnp.int32)[None, :] + 1
    turns = lambda steps: (steps[:, None] * places % (8 * width)).astype(jnp.float32) * (
        math.pi / (4 * width)
    )
    blocks = starts[:, None] + fine * jnp.arange(count // fine, dtype=jnp.int32)[None, :]
    coarse_turn = turns(2 * blocks.reshape(-1))
    fine_turn = turns(2 * jnp.arange(fine, dtype=jnp.int32) + 1)
    trig = [jnp.cos(coarse_turn), jnp.sin(coarse_turn), jnp.cos(fine_turn), jnp.sin(fine_turn)]
    cos_a, sin_a, cos_b, sin_b = lax.optimization_barrier(trig)
    table = cos_a[:, None] * cos_b[None] - sin_a[:, None] * sin_b[None]
    return table.reshape(-1, width).astype(jnp.bfloat16)


def spectra_kernel(late, cuts, scale, core_ref, weights_ref, table_ref, *refs):
    sources = 4 if late else 2
    inputs, outs = refs[:sources], refs[sources:-4]
    samples, folded, spread, sems = refs[-4:]
    core = core_ref[0]
    own, other = inputs[0], inputs[1]
    count, width = folded.shape[1], folded.shape[2]
    depth, frames = weights_ref.shape[0], folded.shape[0]
    slab, tail = frames * width, (depth - 1) * width
    step_rows = count // ROW_STEPS
    half_rows = count // 2

    def slab_copy(ref, step, columns, start, which):
        rows = pl.ds(step * step_rows, step_rows)
        return pltpu.make_async_copy(
            ref.at[rows, pl.ds(0, columns)],
            samples.at[rows, pl.ds(start, columns)],
            sems.at[which, step],
        )

    def halo_copy(ref, step):
        rows = pl.ds(step * step_rows, step_rows)
        return pltpu.make_async_copy(
            ref.at[pl.ds(step * step_rows % half_rows, step_rows), :],
            samples.at[rows, pl.ds(slab, tail)],
            sems.at[1, step],
        )

    def start_all(first, second):
        for step in range(ROW_STEPS):
            slab_copy(first, step, slab, 0, 0).start()
            if not late:
                slab_copy(second, step, tail, slab, 1).start()

    head_core = 1 if late else 0

    @pl.when(core == head_core)
    def _():
        start_all(own, other)

    @pl.when(core != head_core)
    def _():
        start_all(other, own)

    if late:
        for step in range(ROW_STEPS):
            half = step * step_rows // half_rows

            @pl.when(core == half)
            def _():
                halo_copy(inputs[2], step).start()

            @pl.when(core != half)
            def _():
                halo_copy(inputs[3], step).start()

    for step in range(ROW_STEPS):
        slab_copy(own, step, slab, 0, 0).wait()
        if late:
            halo_copy(inputs[2], step).wait()
        else:
            slab_copy(own, step, tail, slab, 1).wait()

        def fold(tile, carry):
            lanes = pl.multiple_of(tile * 128, 128)
            taps = [
                jnp.broadcast_to(weights_ref[pl.ds(tap, 1), pl.ds(lanes, 128)], (16, 128))
                for tap in range(depth)
            ]
            for block in range(step_rows // 16):
                rows = pl.ds(step * step_rows + block * 16, 16)
                window = [
                    samples[rows, pl.ds(pl.multiple_of(lanes + place * width, 128), 128)].astype(
                        jnp.float32
                    )
                    for place in range(frames + depth - 1)
                ]
                for frame in range(frames):
                    total = taps[0] * window[frame]
                    for tap in range(1, depth):
                        total = total + taps[tap] * window[frame + tap]
                    folded[frame, rows, pl.ds(lanes, 128)] = total.astype(jnp.bfloat16)
            return carry

        lax.fori_loop(0, width // 128, fold, 0)

    channels = table_ref.shape[0]
    for frame in range(frames):
        product = scale * lax.dot_general(
            table_ref[...],
            folded[frame],
            (((1,), (1,)), ((), ())),
            preferred_element_type=jnp.float32,
        )
        for half in range(count // 128):
            spread[half, pl.ds(frame, channels, stride=frames), :] = product[
                :, half * 128 : half * 128 + 128
            ]
    for (first, rows), out in zip(cuts, outs):
        for half in range(count // 128):
            out[:, half * 128 : half * 128 + 128] = spread[half, first : first + rows, :].astype(
                jnp.bfloat16
            )


def spectra_blocks(late, cuts, core, weights, table, sources):
    count = sources[0].shape[0]
    depth, width = weights.shape
    frames = sources[0].shape[1] // width
    channels = table.shape[0]
    cuts = [(first * frames, rows * frames) for first, rows in cuts]
    whole = pl.BlockSpec(memory_space=pltpu.VMEM)
    return pl.pallas_call(
        functools.partial(spectra_kernel, late, cuts, math.sqrt(2.0 / width)),
        out_shape=[jax.ShapeDtypeStruct((rows, count), jnp.bfloat16) for _, rows in cuts],
        in_specs=[pl.BlockSpec(memory_space=pltpu.SMEM), whole, whole]
        + [pl.BlockSpec(memory_space=pl.ANY)] * len(sources),
        out_specs=[whole] * len(cuts),
        scratch_shapes=[
            pltpu.VMEM((count, (frames + depth - 1) * width), jnp.bfloat16),
            pltpu.VMEM((frames, count, width), jnp.bfloat16),
            pltpu.VMEM((count // 128, channels * frames, 128), jnp.float32),
            pltpu.SemaphoreType.DMA((2, ROW_STEPS)),
        ],
        compiler_params=pltpu.CompilerParams(vmem_limit_bytes=FOLD_VMEM),
        cost_estimate=pl.CostEstimate(flops=1, bytes_accessed=1, transcendentals=0),
        name="fold_transform",
    )(core, weights, table, *sources)


def correlate_kernel(scale, groups, ordered, first, group_ref, *refs):
    out, held, sems = refs[-3:]
    count = out.shape[1]
    group = group_ref[0]
    step, steps = pl.program_id(0), pl.num_programs(0)
    slot = step % 2
    pieces, used = [], 0
    for is_ordered in ordered:
        members = refs[used : used + (1 if is_ordered else groups)]
        used += len(members)
        pieces += [(is_ordered, members, part) for part in range(members[0].shape[-3])]

    def copy(where, channel):
        target = first + step * 2 * PAIRS + channel
        return pltpu.make_async_copy(held.at[where, channel], out.at[target], sems.at[where, channel])

    def wait_all(where):
        for channel in range(2 * PAIRS):
            copy(where, channel).wait()

    @pl.when(step >= 2)
    def _():
        wait_all(slot)

    depth = len(pieces) * 16
    places = lax.broadcasted_iota(jnp.int32, (count, depth), 1)
    even = jnp.where(places % 16 < 8, scale, 0.0).astype(jnp.bfloat16)
    odd = jnp.where(places % 16 < 8, 0.0, scale).astype(jnp.bfloat16)
    for pair in range(PAIRS):
        rows = slice(pair * 16, pair * 16 + 16)

        def stack(member):
            return jnp.concatenate(
                [
                    members[0][group ^ member, part, rows, :]
                    if is_ordered
                    else members[member][part, rows, :]
                    for is_ordered, members, part in pieces
                ],
                axis=0,
            )

        turned = stack(0).T
        left = jnp.concatenate([turned * even, turned * odd], axis=0)
        for member in range(groups):
            summed = lax.dot_general(
                left, stack(member), (((1,), (0,)), ((), ())), preferred_element_type=jnp.float32
            )
            columns = pl.ds(pl.multiple_of((group ^ member) * count, 128), count)
            result = summed.astype(jnp.bfloat16)
            held[slot, 2 * pair, :, columns] = result[:count]
            held[slot, 2 * pair + 1, :, columns] = result[count:]
        copy(slot, 2 * pair).start()
        copy(slot, 2 * pair + 1).start()

    @pl.when(step == steps - 1)
    def _():
        wait_all(slot)

    @pl.when((step == steps - 1) & (steps > 1))
    def _():
        wait_all(1 - slot)


def correlate(frames, first, stop, channels, group, wide, narrow, earlier):
    groups, count = lax.axis_size("grp"), (wide + narrow)[0][-1].shape[-1]
    block = 2 * PAIRS
    base, steps = first // block, (stop - first) // block
    pieces = [(piece, base) for piece in wide] + [(piece, 0) for piece in narrow]
    ordered = [len(piece) == 1 for piece, _ in pieces]
    operands = [array for piece, _ in pieces for array in piece]
    aliases = {} if earlier is None else {1 + len(operands): 0}
    carried = [] if earlier is None else [earlier]

    def spec(array, start):
        if len(array.shape) == 4:
            return pl.BlockSpec(
                (groups, array.shape[1], 16 * PAIRS, count), lambda i, ref: (0, 0, start + i, 0)
            )
        return pl.BlockSpec((array.shape[0], 16 * PAIRS, count), lambda i, ref: (0, start + i, 0))

    return pl.pallas_call(
        functools.partial(correlate_kernel, 1.0 / frames, groups, ordered, first),
        out_shape=jax.ShapeDtypeStruct((channels, count, groups * count), jnp.bfloat16),
        grid_spec=pltpu.PrefetchScalarGridSpec(
            num_scalar_prefetch=1,
            grid=(steps,),
            in_specs=[spec(array, start) for piece, start in pieces for array in piece]
            + [pl.BlockSpec(memory_space=pl.ANY)] * len(carried),
            out_specs=pl.BlockSpec(memory_space=pl.ANY),
            scratch_shapes=[
                pltpu.VMEM((2, block, count, groups * count), jnp.bfloat16),
                pltpu.SemaphoreType.DMA((2, block)),
            ],
        ),
        input_output_aliases=aliases,
        compiler_params=pltpu.CompilerParams(vmem_limit_bytes=CORRELATE_VMEM),
        cost_estimate=pl.CostEstimate(flops=1, bytes_accessed=1, transcendentals=0),
        name="correlate",
    )(group, *operands, *carried)


def joined(block, turn, earlier=None, events=()):
    groups = lax.axis_size("grp")
    bits = [1 << b for b in range(groups.bit_length() - 1)]
    bits = bits[turn % len(bits) :] + bits[: turn % len(bits)]
    held = {0: block}
    for bit in bits:
        for member in list(held):
            waits = () if earlier is None else (earlier[member | bit],)
            sent = after(held[member], *waits, *(events if member else ()))
            held[member | bit] = swap(sent, "grp", bit)
    return [held[member] for member in range(groups)]


def on_device(voltages, prototype):
    depth, width = prototype.shape
    owners = lax.axis_size("chan")
    parts = owners // 2
    channels = width // owners
    frames_here = voltages.shape[1] // width
    frames = frames_here * owners
    place = lax.axis_index("chan")
    core = place % 2
    group = lax.axis_index("grp")
    half = voltages.shape[0] // 2

    other = swap(voltages, "chan", 1)
    route = [[(2 * p + 2, 2 * p + k) for p in range(parts - 1)] for k in (0, 1)]
    tail = (depth - 1) * width
    sliced = [voltages[k * half : k * half + half, :tail] for k in (0, 1)]
    ahead = [lax.ppermute(sliced[k], "chan", route[k]) for k in (0, 1)]
    other = after(other, *sliced)

    owned = (place // 2) ^ jnp.arange(parts, dtype=jnp.int32)
    table = cosine_rows((owned * 2 + core) * channels, channels, width)
    signs = jnp.where(jnp.arange(depth) % 2 == 0, 1.0, -1.0).astype(jnp.float32)
    weights = signs[:, None] * prototype
    at_core = core.reshape(1)

    cuts = [(part * channels, channels) for part in range(parts)]
    early = spectra_blocks(False, cuts, at_core, weights, table, [voltages, other])
    own_early = joined(early[0][None], 0)
    near = swap(early[1], "chan", 2)
    near_joined = joined(near[None], 1, own_early)
    middle = swap(after(early[2], near), "chan", 4)
    far = [swap(after(early[part], middle), "chan", 2 * part) for part in range(3, parts)]

    ahead = lax.optimization_barrier((ahead[0], ahead[1], near, *own_early[1:]))
    halo = jnp.where(core == 0, ahead[0], ahead[1])
    other_halo = swap(halo, "chan", 1)
    bounds = [round(channels * bound / (32 * PAIRS)) * 2 * PAIRS for bound in BOUNDS]
    blocks = list(zip(bounds[:-1], bounds[1:]))
    cuts = [(0, channels)] + [
        (part * channels + first, stop - first)
        for first, stop in blocks
        for part in range(1, parts)
    ]
    late = spectra_blocks(True, cuts, at_core, weights, table, [voltages, other, halo, other_halo])
    own_late = joined(late[0][None], 0, near_joined)
    middle_joined = joined(middle[None], 1, own_late)
    far_joined = joined(jnp.stack(far), 0, middle_joined)
    wide = [own_early, near_joined, own_late, middle_joined, far_joined]
    landed, narrow, results = [near, middle] + far, [far_joined], [None]
    for chunk, (first, stop) in enumerate(blocks):
        skipped = chunk * (parts - 1)
        landed = [
            swap(after(late[skipped + part], landed[part - 1]), "chan", 2 * part)
            for part in range(1, parts)
        ]
        events = results[chunk - 1 : chunk] if chunk >= 2 else ()
        narrow.append(joined(jnp.stack(landed), chunk + 1, narrow[-1], events))
        results.append(
            correlate(
                frames, first, stop, channels, group.reshape(1), wide, [narrow[-1]], results[-1]
            )
        )
    return results[-1]


def solution(mesh):
    placed = (P("grp", "chan"), P())
    return jax.shard_map(
        on_device, mesh=mesh, in_specs=placed, out_specs=P("chan", "grp", None), check_vma=False
    )
```

```python
import functools
import math

import jax
import jax.numpy as jnp
from jax import lax
from jax.experimental import pallas as pl
from jax.experimental.pallas import tpu as pltpu
from jax.sharding import PartitionSpec as P

BOUNDS = (0, 6, 11, 16)
ROW_STEPS = 4
PAIRS = 4
FOLD_VMEM = 28 * 1024 * 1024
CORRELATE_VMEM = 60 * 1024 * 1024


def swap(block, axis, bit):
    return lax.ppermute(block, axis, [(i, i ^ bit) for i in range(lax.axis_size(axis))])


def after(value, *events):
    return lax.optimization_barrier((value,) + events)[0]


def cosine_rows(starts, count, width):
    fine = math.gcd(count, 32)
    places = 2 * jnp.arange(width, dtype=jnp.int32)[None, :] + 1
    turns = lambda steps: (steps[:, None] * places % (8 * width)).astype(jnp.float32) * (
        math.pi / (4 * width)
    )
    blocks = starts[:, None] + fine * jnp.arange(count // fine, dtype=jnp.int32)[None, :]
    coarse_turn = turns(2 * blocks.reshape(-1))
    fine_turn = turns(2 * jnp.arange(fine, dtype=jnp.int32) + 1)
    trig = [jnp.cos(coarse_turn), jnp.sin(coarse_turn), jnp.cos(fine_turn), jnp.sin(fine_turn)]
    cos_a, sin_a, cos_b, sin_b = lax.optimization_barrier(trig)
    table = cos_a[:, None] * cos_b[None] - sin_a[:, None] * sin_b[None]
    return table.reshape(-1, width).astype(jnp.bfloat16)


def spectra_kernel(late, cuts, scale, core_ref, weights_ref, table_ref, *refs):
    sources = 4 if late else 2
    inputs, outs = refs[:sources], refs[sources:-4]
    samples, folded, spread, sems = refs[-4:]
    core = core_ref[0]
    own, other = inputs[0], inputs[1]
    count, width = folded.shape[1], folded.shape[2]
    depth, frames = weights_ref.shape[0], folded.shape[0]
    slab, tail = frames * width, (depth - 1) * width
    step_rows = count // ROW_STEPS
    half_rows = count // 2

    def slab_copy(ref, step, columns, start, which):
        rows = pl.ds(step * step_rows, step_rows)
        return pltpu.make_async_copy(
            ref.at[rows, pl.ds(0, columns)],
            samples.at[rows, pl.ds(start, columns)],
            sems.at[which, step],
        )

    def halo_copy(ref, step):
        rows = pl.ds(step * step_rows, step_rows)
        return pltpu.make_async_copy(
            ref.at[pl.ds(step * step_rows % half_rows, step_rows), :],
            samples.at[rows, pl.ds(slab, tail)],
            sems.at[1, step],
        )

    def start_all(first, second):
        for step in range(ROW_STEPS):
            slab_copy(first, step, slab, 0, 0).start()
            if not late:
                slab_copy(second, step, tail, slab, 1).start()

    head_core = 1 if late else 0

    @pl.when(core == head_core)
    def _():
        start_all(own, other)

    @pl.when(core != head_core)
    def _():
        start_all(other, own)

    if late:
        for step in range(ROW_STEPS):
            half = step * step_rows // half_rows

            @pl.when(core == half)
            def _():
                halo_copy(inputs[2], step).start()

            @pl.when(core != half)
            def _():
                halo_copy(inputs[3], step).start()

    for step in range(ROW_STEPS):
        slab_copy(own, step, slab, 0, 0).wait()
        if late:
            halo_copy(inputs[2], step).wait()
        else:
            slab_copy(own, step, tail, slab, 1).wait()

        def fold(tile, carry):
            lanes = pl.multiple_of(tile * 128, 128)
            taps = [
                jnp.broadcast_to(weights_ref[pl.ds(tap, 1), pl.ds(lanes, 128)], (16, 128))
                for tap in range(depth)
            ]
            for block in range(step_rows // 16):
                rows = pl.ds(step * step_rows + block * 16, 16)
                window = [
                    samples[rows, pl.ds(pl.multiple_of(lanes + place * width, 128), 128)].astype(
                        jnp.float32
                    )
                    for place in range(frames + depth - 1)
                ]
                for frame in range(frames):
                    total = taps[0] * window[frame]
                    for tap in range(1, depth):
                        total = total + taps[tap] * window[frame + tap]
                    folded[frame, rows, pl.ds(lanes, 128)] = total.astype(jnp.bfloat16)
            return carry

        lax.fori_loop(0, width // 128, fold, 0)

    channels = table_ref.shape[0]
    for frame in range(frames):
        product = scale * lax.dot_general(
            table_ref[...],
            folded[frame],
            (((1,), (1,)), ((), ())),
            preferred_element_type=jnp.float32,
        )
        for half in range(count // 128):
            spread[half, pl.ds(frame, channels, stride=frames), :] = product[
                :, half * 128 : half * 128 + 128
            ]
    for (first, rows), out in zip(cuts, outs):
        for half in range(count // 128):
            out[:, half * 128 : half * 128 + 128] = spread[half, first : first + rows, :].astype(
                jnp.bfloat16
            )


def spectra_blocks(late, cuts, core, weights, table, sources):
    count = sources[0].shape[0]
    depth, width = weights.shape
    frames = sources[0].shape[1] // width
    channels = table.shape[0]
    cuts = [(first * frames, rows * frames) for first, rows in cuts]
    whole = pl.BlockSpec(memory_space=pltpu.VMEM)
    return pl.pallas_call(
        functools.partial(spectra_kernel, late, cuts, math.sqrt(2.0 / width)),
        out_shape=[jax.ShapeDtypeStruct((rows, count), jnp.bfloat16) for _, rows in cuts],
        in_specs=[pl.BlockSpec(memory_space=pltpu.SMEM), whole, whole]
        + [pl.BlockSpec(memory_space=pl.ANY)] * len(sources),
        out_specs=[whole] * len(cuts),
        scratch_shapes=[
            pltpu.VMEM((count, (frames + depth - 1) * width), jnp.bfloat16),
            pltpu.VMEM((frames, count, width), jnp.bfloat16),
            pltpu.VMEM((count // 128, channels * frames, 128), jnp.float32),
            pltpu.SemaphoreType.DMA((2, ROW_STEPS)),
        ],
        compiler_params=pltpu.CompilerParams(vmem_limit_bytes=FOLD_VMEM),
        cost_estimate=pl.CostEstimate(flops=1, bytes_accessed=1, transcendentals=0),
        name="fold_transform",
    )(core, weights, table, *sources)


def correlate_kernel(scale, groups, ordered, first, group_ref, *refs):
    out, held, sems = refs[-3:]
    count = out.shape[1]
    group = group_ref[0]
    step, steps = pl.program_id(0), pl.num_programs(0)
    slot = step % 2
    pieces, used = [], 0
    for is_ordered in ordered:
        members = refs[used : used + (1 if is_ordered else groups)]
        used += len(members)
        pieces += [(is_ordered, members, part) for part in range(members[0].shape[-3])]

    def copy(where, channel):
        target = first + step * 2 * PAIRS + channel
        return pltpu.make_async_copy(held.at[where, channel], out.at[target], sems.at[where, channel])

    def wait_all(where):
        for channel in range(2 * PAIRS):
            copy(where, channel).wait()

    @pl.when(step >= 2)
    def _():
        wait_all(slot)

    depth = len(pieces) * 16
    places = lax.broadcasted_iota(jnp.int32, (count, depth), 1)
    even = jnp.where(places % 16 < 8, scale, 0.0).astype(jnp.bfloat16)
    odd = jnp.where(places % 16 < 8, 0.0, scale).astype(jnp.bfloat16)
    for pair in range(PAIRS):
        rows = slice(pair * 16, pair * 16 + 16)

        def stack(member):
            return jnp.concatenate(
                [
                    members[0][group ^ member, part, rows, :]
                    if is_ordered
                    else members[member][part, rows, :]
                    for is_ordered, members, part in pieces
                ],
                axis=0,
            )

        turned = stack(0).T
        left = jnp.concatenate([turned * even, turned * odd], axis=0)
        for member in range(groups):
            summed = lax.dot_general(
                left, stack(member), (((1,), (0,)), ((), ())), preferred_element_type=jnp.float32
            )
            columns = pl.ds(pl.multiple_of((group ^ member) * count, 128), count)
            result = summed.astype(jnp.bfloat16)
            held[slot, 2 * pair, :, columns] = result[:count]
            held[slot, 2 * pair + 1, :, columns] = result[count:]
        copy(slot, 2 * pair).start()
        copy(slot, 2 * pair + 1).start()

    @pl.when(step == steps - 1)
    def _():
        wait_all(slot)

    @pl.when((step == steps - 1) & (steps > 1))
    def _():
        wait_all(1 - slot)


def correlate(frames, first, stop, channels, group, wide, parted, narrow, earlier):
    groups, count = lax.axis_size("grp"), (wide + narrow)[0][-1].shape[-1]
    block = 2 * PAIRS
    base, steps = first // block, (stop - first) // block
    pieces = [(piece, base) for piece in wide] + [(piece, 0) for piece in narrow]
    pieces.append((parted[0], (first - parted[1]) // block))
    ordered = [len(piece) == 1 for piece, _ in pieces]
    operands = [array for piece, _ in pieces for array in piece]
    aliases = {} if earlier is None else {1 + len(operands): 0}
    carried = [] if earlier is None else [earlier]

    def spec(array, start):
        if len(array.shape) == 4:
            return pl.BlockSpec(
                (groups, array.shape[1], 16 * PAIRS, count), lambda i, ref: (0, 0, start + i, 0)
            )
        return pl.BlockSpec((array.shape[0], 16 * PAIRS, count), lambda i, ref: (0, start + i, 0))

    return pl.pallas_call(
        functools.partial(correlate_kernel, 1.0 / frames, groups, ordered, first),
        out_shape=jax.ShapeDtypeStruct((channels, count, groups * count), jnp.bfloat16),
        grid_spec=pltpu.PrefetchScalarGridSpec(
            num_scalar_prefetch=1,
            grid=(steps,),
            in_specs=[spec(array, start) for piece, start in pieces for array in piece]
            + [pl.BlockSpec(memory_space=pl.ANY)] * len(carried),
            out_specs=pl.BlockSpec(memory_space=pl.ANY),
            scratch_shapes=[
                pltpu.VMEM((2, block, count, groups * count), jnp.bfloat16),
                pltpu.SemaphoreType.DMA((2, block)),
            ],
        ),
        input_output_aliases=aliases,
        compiler_params=pltpu.CompilerParams(vmem_limit_bytes=CORRELATE_VMEM),
        cost_estimate=pl.CostEstimate(flops=1, bytes_accessed=1, transcendentals=0),
        name="correlate",
    )(group, *operands, *carried)


def joined(block, turn, earlier=None, events=()):
    groups = lax.axis_size("grp")
    bits = [1 << b for b in range(groups.bit_length() - 1)]
    bits = bits[turn % len(bits) :] + bits[: turn % len(bits)]
    held = {0: block}
    for bit in bits:
        for member in list(held):
            waits = () if earlier is None else (earlier[member | bit],)
            sent = after(held[member], *waits, *(events if member else ()))
            held[member | bit] = swap(sent, "grp", bit)
    return [held[member] for member in range(groups)]


def on_device(voltages, prototype):
    depth, width = prototype.shape
    owners = lax.axis_size("chan")
    parts = owners // 2
    channels = width // owners
    frames_here = voltages.shape[1] // width
    frames = frames_here * owners
    place = lax.axis_index("chan")
    core = place % 2
    group = lax.axis_index("grp")
    half = voltages.shape[0] // 2

    other = swap(voltages, "chan", 1)
    route = [[(2 * p + 2, 2 * p + k) for p in range(parts - 1)] for k in (0, 1)]
    tail = (depth - 1) * width
    sliced = [voltages[k * half : k * half + half, :tail] for k in (0, 1)]
    ahead = [lax.ppermute(sliced[k], "chan", route[k]) for k in (0, 1)]
    other = after(other, *sliced)

    owned = (place // 2) ^ jnp.arange(parts, dtype=jnp.int32)
    table = cosine_rows((owned * 2 + core) * channels, channels, width)
    signs = jnp.where(jnp.arange(depth) % 2 == 0, 1.0, -1.0).astype(jnp.float32)
    weights = signs[:, None] * prototype
    at_core = core.reshape(1)

    bounds = [round(channels * bound / (32 * PAIRS)) * 2 * PAIRS for bound in BOUNDS]
    head = bounds[1]
    cuts = [(0, channels), (channels, head), (channels + head, channels - head)]
    cuts += [(part * channels, channels) for part in range(2, parts)]
    early = spectra_blocks(False, cuts, at_core, weights, table, [voltages, other])
    own_early = joined(early[0][None], 0)
    near, near_rest = swap(early[1], "chan", 2), swap(early[2], "chan", 2)
    near_joined = joined(near[None], 1, own_early)
    rest_joined = joined(near_rest[None], 1, near_joined)
    middle = swap(after(early[3], near_rest), "chan", 4)
    far = [swap(after(early[part + 1], middle), "chan", 2 * part) for part in range(3, parts)]

    ahead = lax.optimization_barrier((ahead[0], ahead[1], near, *own_early[1:]))
    halo = jnp.where(core == 0, ahead[0], ahead[1])
    other_halo = after(swap(halo, "chan", 1), near_rest)
    blocks = list(zip(bounds[:-1], bounds[1:]))
    cuts = [(0, channels)] + [
        (part * channels + first, stop - first)
        for first, stop in blocks
        for part in range(1, parts)
    ]
    late = spectra_blocks(True, cuts, at_core, weights, table, [voltages, other, halo, other_halo])
    own_late = joined(late[0][None], 0, rest_joined)
    middle_joined = joined(middle[None], 1, own_late)
    far_joined = joined(jnp.stack(far), 0, middle_joined)
    wide = [own_early, own_late, middle_joined, far_joined]
    landed, narrow, results = [near_rest, middle] + far, [far_joined], [None]
    for chunk, (first, stop) in enumerate(blocks):
        skipped = chunk * (parts - 1)
        landed = [
            swap(after(late[skipped + part], landed[part - 1]), "chan", 2 * part)
            for part in range(1, parts)
        ]
        events = results[chunk - 1 : chunk] if chunk >= 2 else ()
        parted = (near_joined, 0) if stop <= head else (rest_joined, head)
        narrow.append(joined(jnp.stack(landed), chunk + 1, narrow[-1], events))
        results.append(
            correlate(
                frames, first, stop, channels, group.reshape(1), wide, parted, [narrow[-1]], results[-1]
            )
        )
    return results[-1]


def solution(mesh):
    placed = (P("grp", "chan"), P())
    return jax.shard_map(
        on_device, mesh=mesh, in_specs=placed, out_specs=P("chan", "grp", None), check_vma=False
    )
```
